32 devices in a mesh: dp: 2 (over x), seq: 4 (over y, core), head: 4 (over z).
Axes of the slice: x: 2, y: 2, z: 4, core: 2. Of those that a mesh axis runs over, the one named last changes fastest.
Arguments:
- x_in: bfloat16 [2, 3072, 4096], P('dp', 'seq', 'head'), may hold values from -6 to 6
- b_in: bfloat16 [2, 3072, 1024], P('dp', 'seq', 'head'), may hold values from -6 to 6
- c_in: bfloat16 [2, 3072, 1024], P('dp', 'seq', 'head'), may hold values from -6 to 6
- z_in: bfloat16 [2, 3072, 4096], P('dp', 'seq', 'head'), may hold values from -24 to 24
- dt_in: float32 [2, 64, 3072], P('dp', 'head', 'seq'), may hold values from -10 to 4.5
- a_log: float32 [64], P('head'), may hold values from -2.3 to 0.58
- skip_gain: float32 [64], P('head'), may hold values from 0.5 to 1.5
- norm_gain: float32 [4096], P('head'), may hold values from 0.5 to 1.5
- conv_x: float32 [4, 4096], P(None, 'head'), may hold values from -3 to 3
- conv_b: float32 [4, 1024], P(None, 'head'), may hold values from -3 to 3
- conv_c: float32 [4, 1024], P(None, 'head'), may hold values from -3 to 3
- init_state: float32 [2, 64, 64, 128], P('dp', 'head'), may hold values from -0.5 to 0.5
- out_weight: bfloat16 [4096, 8192], P(('dp', 'seq'), 'head'), may hold values from -0.09375 to 0.09375
Outputs:
- mixed: bfloat16 [2, 3072, 8192], P('dp', 'seq', 'head')
The draws below stay inside these ranges and needn't reach their ends.
All inputs are finite; a program needn't handle non-finite values.
Results may differ from the reference program's by a relative error of at most 0.0058.
Values may be sent and summed in bfloat16 or wider, within the bound.
A program may use at most 128 MiB of HBM per device.

```python
import math
import jax
import jax.numpy as jnp
from jax import lax

D = 8192
HEAD_SIZE = 64
STATE = 128
BLOCK_LEN = 256
TAPS = 4
TOK_DEV = 768
SSM_HEAD_COUNT = 64
GROUPS = 8
SEQ_LEN = 3072
ROLLOUT_COUNT = 2


def fast_heads(key):
    chooser = jax.random.fold_in(key, 101)
    fast_share = 0.5
    return jax.random.uniform(chooser, (SSM_HEAD_COUNT,)) < fast_share


def head_log_rates(key):
    fast_mask = fast_heads(key)
    jitter = jax.random.uniform(jax.random.fold_in(key, 202), (SSM_HEAD_COUNT,), jnp.float32, -0.35, 0.35)
    slow_level = jax.random.uniform(jax.random.fold_in(key, 212), (SSM_HEAD_COUNT,), jnp.float32, -2.3, -1.6)
    return jnp.where(fast_mask, math.log(1.25) + jitter, slow_level).astype(jnp.float32)


def draw_a_log(key, part):
    return head_log_rates(key)


def draw_dt_in(key, part):
    fast_mask = fast_heads(key)[None, :, None]
    rates = jnp.exp(head_log_rates(key))[None, :, None]
    blocks = SEQ_LEN // TOK_DEV
    jitter_tok = jax.random.uniform(jax.random.fold_in(key, 303), (ROLLOUT_COUNT, SSM_HEAD_COUNT, blocks, TOK_DEV), jnp.float32, -0.7, 0.7)
    offset = jax.random.uniform(jax.random.fold_in(key, 404), (ROLLOUT_COUNT, SSM_HEAD_COUNT, blocks, 1), jnp.float32, -0.4, 0.4)
    noisy_portion = (jitter_tok + offset).reshape(ROLLOUT_COUNT, SSM_HEAD_COUNT, SEQ_LEN)
    target = jax.random.uniform(jax.random.fold_in(key, 313), (ROLLOUT_COUNT, SSM_HEAD_COUNT, 1), jnp.float32, 1.0, 1.5)
    slow_level = jnp.log(target / (SEQ_LEN * rates))
    baseline_level = jnp.where(fast_mask, math.log(0.02), slow_level)
    location_list = jax.random.randint(jax.random.fold_in(key, 505), (ROLLOUT_COUNT, 2), 0, SEQ_LEN)
    token_position = jnp.arange(SEQ_LEN)
    spike_mask = jnp.any(token_position[None, None, :] == location_list[:, :, None], axis=1)[:, None, :]
    loss_share = jax.random.uniform(jax.random.fold_in(key, 606), (ROLLOUT_COUNT, SSM_HEAD_COUNT, 1), jnp.float32, 0.2, 0.35)
    spike_step = -jnp.log1p(-loss_share) / rates
    spike_value = jnp.log(jnp.expm1(spike_step))
    return jnp.where(spike_mask, spike_value, baseline_level + noisy_portion).astype(jnp.float32)


def draw_z_in(key, part):
    shape_full = (ROLLOUT_COUNT, SEQ_LEN, SSM_HEAD_COUNT * HEAD_SIZE)
    column = jnp.exp(jax.random.uniform(jax.random.fold_in(key, 707), (SSM_HEAD_COUNT * HEAD_SIZE,), jnp.float32, math.log(0.3), math.log(3.0)))
    row_scale = jnp.exp(jax.random.uniform(jax.random.fold_in(key, 808), (ROLLOUT_COUNT, SEQ_LEN, 1), jnp.float32, math.log(0.5), math.log(2.0)))
    values = jax.random.truncated_normal(jax.random.fold_in(key, 909), -4.0, 4.0, shape_full, jnp.float32)
    return (values * column * row_scale).astype(jnp.bfloat16)


def steps_of(key, shape, split, low, largest):
    factor_of, own = 1.0, jax.random.fold_in(key, 6)
    for dim, parts in split:
        steps = jnp.exp(jax.random.uniform(jax.random.fold_in(own, dim), (parts,), jnp.float32, low / len(split), largest / len(split)))
        factor_of = factor_of * jnp.repeat(steps, shape[dim] // parts).reshape([-1 if axis == dim else 1 for axis in range(len(shape))])
    return factor_of


def gaussian(own_key, shape, scale, bound, pieces=(), dtype=jnp.bfloat16):
    loudness = steps_of(own_key, shape, pieces, -0.22, 0.18) if pieces else 1.0
    result = jax.random.normal(own_key, shape, jnp.float32) * scale * loudness
    return jnp.minimum(jnp.maximum(result, -bound), bound).astype(dtype)


def setup_inputs(seed: int = 0) -> dict:
    streams_of = jax.random.split(jax.random.key(seed), 14)
    x_in = gaussian(streams_of[0], (ROLLOUT_COUNT, SEQ_LEN, SSM_HEAD_COUNT * HEAD_SIZE), 1.0, 6.0, ((0, 2), (1, 4), (2, 4)))
    b_in = gaussian(streams_of[1], (ROLLOUT_COUNT, SEQ_LEN, GROUPS * STATE), 1.0, 6.0, ((0, 2), (1, 4), (2, 4)))
    c_in = gaussian(streams_of[2], (ROLLOUT_COUNT, SEQ_LEN, GROUPS * STATE), 1.0, 6.0, ((0, 2), (1, 4), (2, 4)))
    z_in = draw_z_in(jax.random.fold_in(streams_of[13], 71), 0)
    dt_in = draw_dt_in(jax.random.fold_in(streams_of[13], 71), 0)
    a_log = draw_a_log(jax.random.fold_in(streams_of[13], 71), 0)
    skip_gain = jnp.clip(0.5 + 1.0 * jax.random.uniform(streams_of[6], (SSM_HEAD_COUNT,), jnp.float32) ** steps_of(streams_of[6], (SSM_HEAD_COUNT,), ((0, 4),), -0.2, 0.2), 0.5, 1.5)
    norm_gain = jnp.clip(1.0 + 0.1 * jax.random.normal(streams_of[7], (SSM_HEAD_COUNT * HEAD_SIZE,), jnp.float32), 0.5, 1.5)
    conv_x = gaussian(streams_of[8], (TAPS, SSM_HEAD_COUNT * HEAD_SIZE), TAPS ** -0.5, 3.0, ((1, 4),), jnp.float32)
    conv_b = gaussian(streams_of[9], (TAPS, GROUPS * STATE), TAPS ** -0.5, 3.0, ((1, 4),), jnp.float32)
    conv_c = gaussian(streams_of[10], (TAPS, GROUPS * STATE), TAPS ** -0.5, 3.0, ((1, 4),), jnp.float32)
    init_state = gaussian(streams_of[11], (ROLLOUT_COUNT, SSM_HEAD_COUNT, HEAD_SIZE, STATE), 0.08, 0.5, ((0, 2), (1, 4)), jnp.float32)
    out_weight = gaussian(streams_of[12], (SSM_HEAD_COUNT * HEAD_SIZE, D), (SSM_HEAD_COUNT * HEAD_SIZE) ** -0.5, 0.09375, ((0, 8), (1, 4)))
    return {"x_in": x_in, "b_in": b_in, "c_in": c_in, "z_in": z_in, "dt_in": dt_in, "a_log": a_log, "skip_gain": skip_gain, "norm_gain": norm_gain, "conv_x": conv_x, "conv_b": conv_b, "conv_c": conv_c, "init_state": init_state, "out_weight": out_weight}


EPSILON = 1e-05

def causal_conv(signal, before, weight):
    joined = jnp.concatenate([before, signal], axis=1).astype(jnp.float32)
    length = signal.shape[1]
    tap_count = weight.shape[0]
    accum_total = weight[0] * joined[:, 0:length]
    for offset in range(1, tap_count):
        accum_total = accum_total + weight[offset] * joined[:, offset:offset + length]
    return jax.nn.silu(accum_total).astype(jnp.bfloat16)

def to_narrow(value):
    return lax.optimization_barrier(value.astype(jnp.bfloat16)).astype(jnp.float32)

def reference(x_in, b_in, c_in, z_in, dt_in, a_log, skip_gain, norm_gain, conv_x, conv_b, conv_c, init_state, out_weight):
    highest = lax.Precision.HIGHEST
    rim_width = TAPS - 1
    roll_count = x_in.shape[0]
    x_conv = causal_conv(x_in, jnp.zeros((roll_count, rim_width, x_in.shape[2]), jnp.bfloat16), conv_x)
    b_conv = causal_conv(b_in, jnp.zeros((roll_count, rim_width, b_in.shape[2]), jnp.bfloat16), conv_b)
    c_conv = causal_conv(c_in, jnp.zeros((roll_count, rim_width, c_in.shape[2]), jnp.bfloat16), conv_c)
    per_group = SSM_HEAD_COUNT // GROUPS
    block_count = SEQ_LEN // BLOCK_LEN
    step_size = jax.nn.softplus(dt_in)
    log_decay = step_size * (-jnp.exp(a_log))[None, :, None]

    def to_blocks(data, inner):
        return jnp.moveaxis(data.reshape((roll_count, block_count, BLOCK_LEN) + inner), 1, 0)
    x_blocks = to_blocks(x_conv, (GROUPS, per_group, HEAD_SIZE))
    b_blocks = to_blocks(b_conv, (GROUPS, STATE))
    c_blocks = to_blocks(c_conv, (GROUPS, STATE))
    dt_blocks = jnp.moveaxis(step_size.reshape(roll_count, GROUPS, per_group, block_count, BLOCK_LEN), 3, 0)
    decay_blocks = jnp.moveaxis(log_decay.reshape(roll_count, GROUPS, per_group, block_count, BLOCK_LEN), 3, 0)
    skip_shaped = skip_gain.reshape(GROUPS, per_group)[:, :, None]
    query_pos = lax.broadcasted_iota(jnp.int32, (BLOCK_LEN, BLOCK_LEN), 0)
    key_pos = lax.broadcasted_iota(jnp.int32, (BLOCK_LEN, BLOCK_LEN), 1)
    causal = query_pos >= key_pos

    def advance(state, inputs):
        x_block, b_block, c_block, dt_block, decay_block = inputs
        x_float = x_block.astype(jnp.float32)
        b_float = b_block.astype(jnp.float32)
        c_float = c_block.astype(jnp.float32)
        cum_decay = jnp.cumsum(decay_block, axis=-1)
        scores = jnp.einsum('rqgn,rsgn->rgqs', c_float, b_float, precision=highest)
        spread = cum_decay[..., :, None] - cum_decay[..., None, :]
        decay_mat = jnp.where(causal, jnp.exp(jnp.minimum(spread, 0.0)), jnp.float32(0.0))
        mixing = to_narrow(scores[:, :, None] * decay_mat * dt_block[..., None, :])
        intra_out = jnp.einsum('rgkqs,rsgkp->rqgkp', mixing, x_float, precision=highest)
        inter_out = jnp.einsum('rqgn,rgkpn->rqgkp', c_float, state, precision=highest)
        inter_out = inter_out * jnp.transpose(jnp.exp(cum_decay), (0, 3, 1, 2))[..., None]
        last_decay = cum_decay[..., -1:]
        weights_in = jnp.exp(last_decay - cum_decay) * dt_block
        weighted = to_narrow(jnp.transpose(weights_in, (0, 3, 1, 2))[..., None] * x_float)
        fresh = jnp.einsum('rsgkp,rsgn->rgkpn', weighted, b_float, precision=highest)
        new_state = jnp.exp(last_decay)[..., None] * state + fresh
        return (new_state, intra_out + inter_out + skip_shaped * x_float)
    start_state = init_state.reshape(roll_count, GROUPS, per_group, HEAD_SIZE, STATE)
    final_state, outputs = lax.scan(advance, start_state, (x_blocks, b_blocks, c_blocks, dt_blocks, decay_blocks))
    ssm_out = jnp.moveaxis(outputs, 0, 1).reshape(roll_count, SEQ_LEN, GROUPS, per_group * HEAD_SIZE)
    gate_act = jax.nn.silu(z_in.astype(jnp.float32)).reshape(roll_count, SEQ_LEN, GROUPS, per_group * HEAD_SIZE)
    gated_out = ssm_out * gate_act
    mean_sq = lax.optimization_barrier(jnp.mean(gated_out * gated_out, axis=-1, keepdims=True))
    normed = gated_out * lax.rsqrt(mean_sq + EPSILON) * norm_gain.reshape(GROUPS, per_group * HEAD_SIZE)
    normed = normed.astype(jnp.bfloat16).reshape(roll_count, SEQ_LEN, SSM_HEAD_COUNT * HEAD_SIZE)

    def project_roll(normed_roll):
        return jnp.dot(normed_roll, out_weight, preferred_element_type=jnp.float32).astype(jnp.bfloat16)
    return lax.map(project_roll, normed)
```

```python
import functools

import jax
import jax.numpy as jnp
from jax import lax
from jax.experimental import pallas as pl
from jax.experimental.pallas import tpu as pltpu
from jax.sharding import PartitionSpec as P

HEAD_SIZE = 64
STATE = 128
BLOCK_LEN = 256
TAPS = 4
EPSILON = 1e-05
RIM = 16

F32 = jnp.float32
BF16 = jnp.bfloat16
MESH = pl.DeviceIdType.MESH
HIGHEST = lax.Precision.HIGHEST


def dot(a, b, dims=((1,), (0,)), precision=None):
    return lax.dot_general(a, b, (dims, ((), ())), precision=precision, preferred_element_type=F32)


def split(v):
    hi = v.astype(BF16)
    return hi, (v - hi.astype(F32)).astype(BF16)


def silu(v):
    return v / (1.0 + jnp.exp(-v))


def kernel(
    sizes,
    x_hbm, b_hbm, c_hbm, z_hbm, w_hbm, dt_ref, a_ref, skip_ref, gain_ref, kx_ref, kb_ref, kc_ref, init_ref,
    out_ref,
    w_all, n_all, xpad, bpad, cpad, z_v, xc, bc, cc, y_v, states, e_in, e_out, dt_row, cum_row, dt_col, cum_col,
    decay, acc,
    load_sem, halo_send, halo_recv, w_send, w_recv, p_send, e_send, e_recv, up_sem, down_sem, n_recv,
):
    D, S, H = sizes
    T = z_v.shape[0]
    G = n_all.shape[1]
    NB = T // BLOCK_LEN
    R = G * NB
    L = BLOCK_LEN
    heads = dt_row.shape[1]
    per = heads // G
    wide = per * HEAD_SIZE
    rows = w_hbm.shape[0]
    M = w_all.shape[1]
    dp, seq, h = lax.axis_index("dp"), lax.axis_index("seq"), lax.axis_index("head")
    SC = S // 2
    NQ = D * SC
    core = lax.rem(seq, 2)
    q = dp * SC + seq // 2
    me = dp * S + seq
    sibling = seq + 1 - 2 * core

    def local(src, dst, i):
        return pltpu.make_async_copy(src, dst, load_sem.at[i])

    loads = [
        local(x_hbm.at[0], xpad.at[pl.ds(RIM, T)], 0),
        local(b_hbm.at[0], bpad.at[pl.ds(RIM, T)], 1),
        local(c_hbm.at[0], cpad.at[pl.ds(RIM, T)], 2),
        local(z_hbm.at[0], z_v, 3),
        local(w_hbm, w_all.at[pl.ds(pl.multiple_of(me * rows, rows), rows)], 4),
    ]
    for copy in loads:
        copy.start()

    barrier = pltpu.get_barrier_semaphore()
    for k in range(1, D * S):
        other = lax.rem(me + k, D * S)
        pl.semaphore_signal(
            barrier, inc=1, device_id={"dp": other // S, "seq": lax.rem(other, S)}, device_id_type=MESH
        )

    for k in (1, H - 1):
        pl.semaphore_signal(barrier, inc=1, device_id={"head": lax.rem(h + k, H)}, device_id_type=MESH)
    pl.semaphore_wait(barrier, D * S + 1)

    halos = [
        pltpu.make_async_remote_copy(
            src_ref=src.at[0, pl.ds(T - RIM, RIM)],
            dst_ref=dst.at[pl.ds(0, RIM)],
            send_sem=halo_send.at[i],
            recv_sem=halo_recv.at[i],
            device_id={"seq": lax.rem(seq + 1, S)},
            device_id_type=MESH,
        )
        for i, (src, dst) in enumerate(((x_hbm, xpad), (b_hbm, bpad), (c_hbm, cpad)))
    ]
    for copy in halos:

        @pl.when(seq < S - 1)
        def _(copy=copy):
            copy.start()

    def w_rows(owner):
        return w_all.at[pl.ds(pl.multiple_of(owner * rows, rows), rows)]

    def owner_of(chip, on):
        return (chip // SC) * S + lax.rem(chip, SC) * 2 + on

    def w_push(k):
        chip = lax.rem(q + k, NQ)
        return pltpu.make_async_remote_copy(
            src_ref=w_hbm,
            dst_ref=w_rows(me),
            send_sem=w_send.at[k],
            recv_sem=w_recv.at[me],
            device_id={"dp": chip // SC, "seq": lax.rem(chip, SC) * 2 + core},
            device_id_type=MESH,
        )

    def w_pair(k, src=None):
        chip = lax.rem(q + NQ - k, NQ)
        owner = owner_of(chip, core)
        return pltpu.make_async_remote_copy(
            src_ref=w_rows(owner) if src is None else src,
            dst_ref=w_rows(owner),
            send_sem=p_send.at[k],
            recv_sem=w_recv.at[owner],
            device_id={"seq": sibling},
            device_id_type=MESH,
        )

    def w_arrived(owner):
        return pltpu.make_async_remote_copy(
            src_ref=w_hbm,
            dst_ref=w_rows(owner),
            send_sem=w_send.at[0],
            recv_sem=w_recv.at[owner],
            device_id={"seq": sibling},
            device_id_type=MESH,
        )

    first = [k for k in range(1, NQ) if k % SC == 0]
    later = [k for k in range(1, NQ) if k % SC != 0]
    for k in first:
        w_push(k).start()

    lane = lax.broadcasted_iota(jnp.int32, (L, L), 1)
    line = lax.broadcasted_iota(jnp.int32, (L, L), 0)
    eye = jnp.where(lane == line, 1.0, 0.0).astype(F32)
    low = jnp.where(lane <= line, 1.0, 0.0).astype(F32)
    rate = -jnp.exp(a_ref[...])
    for b in range(NB):
        raw = dt_ref[0, :, b * L : (b + 1) * L]
        step = jnp.maximum(raw, 0.0) + jnp.log1p(jnp.exp(-jnp.abs(raw)))
        dt_row[b] = step
        step_c = dot(eye, step, ((1,), (1,)), HIGHEST)
        cum = dot(low, step_c * rate, precision=HIGHEST)
        dt_col[b * L : (b + 1) * L] = step_c
        cum_col[b * L : (b + 1) * L] = cum
        cum_row[b] = dot(cum, eye, ((0,), (0,)), HIGHEST)

    def spread_mat(g):
        head = lax.broadcasted_iota(jnp.int32, (heads, wide), 0)
        chan = lax.broadcasted_iota(jnp.int32, (heads, wide), 1)
        inside = (chan >= (head - g * per) * HEAD_SIZE) & (chan < (head - g * per + 1) * HEAD_SIZE)
        return jnp.where(inside, 1.0, 0.0).astype(BF16)

    def expand(v, mat):
        hi, lo = split(v)
        return dot(hi, mat) + dot(lo, mat)

    for i in range(3):
        loads[i].wait()
    for copy, pad in zip(halos, (xpad, bpad, cpad)):

        @pl.when(seq > 0)
        def _(copy=copy):
            copy.wait_recv()

        @pl.when(seq == 0)
        def _(pad=pad):
            pad[0:RIM] = jnp.zeros((RIM, pad.shape[1]), BF16)

    def conv(pad, taps, dst, b, at):
        v = pad[pl.ds(pl.multiple_of(b * L, L), L + RIM), at : at + 128].astype(F32)
        total = v * taps[TAPS - 1 : TAPS, at : at + 128]
        for back in range(1, TAPS):
            total = total + pltpu.roll(v, back, 0) * taps[TAPS - 1 - back : TAPS - back, at : at + 128]
        dst[pl.ds(pl.multiple_of(b * L, L), L), at : at + 128] = silu(total[RIM:]).astype(BF16)

    def e_copy(g):
        return pltpu.make_async_remote_copy(
            src_ref=e_out.at[g],
            dst_ref=e_in.at[g],
            send_sem=e_send.at[g],
            recv_sem=e_recv.at[g],
            device_id={"seq": lax.rem(seq + 1, S)},
            device_id_type=MESH,
        )

    for g in range(G):
        mat = spread_mat(g)

        def block(b, carry, g=g, mat=mat):
            here = pl.ds(pl.multiple_of(b * L, L), L)
            conv(bpad, kb_ref, bc, b, g * STATE)
            for at in range(g * wide, (g + 1) * wide, 128):
                conv(xpad, kx_ref, xc, b, at)
            cum = cum_col[here]
            last = cum[L - 1 : L]
            weight = expand(jnp.exp(last - cum) * dt_col[here], mat)
            weighted = (weight * xc[here, g * wide : (g + 1) * wide].astype(F32)).astype(BF16)
            states[b, g] = dot(bc[here, g * STATE : (g + 1) * STATE], weighted, ((0,), (0,)))
            decay[b, g] = expand(jnp.broadcast_to(jnp.exp(last), (8, heads)), mat)
            return carry

        lax.fori_loop(0, NB, block, 0)

        @pl.when(seq == 0)
        def _(g=g):
            e_in[g] = init_ref[g * wide : (g + 1) * wide].T

        @pl.when(seq > 0)
        def _(g=g):
            e_copy(g).wait_recv()

        def chain(i, carry, g=g):
            at = pl.ds(pl.multiple_of(i * 32, 32), 32)
            run = e_in[g, at]
            for b in range(NB):
                fresh = states[b, g, at]
                states[b, g, at] = run
                run = decay[b, g, 0:1] * run + fresh
            e_out[g, at] = run
            return carry

        lax.fori_loop(0, STATE // 32, chain, 0)

        @pl.when(seq < S - 1)
        def _(g=g):
            e_copy(g).start()

    for k in later:
        w_push(k).start()
    w_pair(0, w_hbm).start()

    def chunk(s, r):
        return n_all.at[s, r // NB, pl.ds(pl.multiple_of(lax.rem(r, NB) * L, L), L)]

    def pass_up(s, r):
        return pltpu.make_async_remote_copy(
            src_ref=chunk(s, r), dst_ref=chunk(s, r), send_sem=up_sem.at[s, r], recv_sem=n_recv.at[s, r],
            device_id={"head": lax.rem(h + 1, H)}, device_id_type=MESH,
        )

    def pass_down(s, r):
        return pltpu.make_async_remote_copy(
            src_ref=chunk(s, r), dst_ref=chunk(s, r), send_sem=down_sem.at[s, r], recv_sem=n_recv.at[s, r],
            device_id={"head": lax.rem(h + H - 1, H)}, device_id_type=MESH,
        )

    def send_own(r):
        @pl.when(h < H - 1)
        def _():
            pass_up(h, r).start()

        @pl.when(h > 0)
        def _():
            pass_down(h, r).start()

    def forward(r):
        for d in range(1, H - 1):
            back = r - d
            ok = (back >= 0) & (back < R)

            @pl.when(ok & (h - d >= 0) & (h < H - 1))
            def _(d=d, back=back):
                copy = pass_up(h - d, back)
                copy.wait_recv()
                copy.start()

            @pl.when(ok & (h + d < H) & (h > 0))
            def _(d=d, back=back):
                copy = pass_down(h + d, back)
                copy.wait_recv()
                copy.start()

    loads[3].wait()
    side = lax.broadcasted_iota(jnp.int32, (L, 128), 1) < HEAD_SIZE
    for g in range(G):
        mat = spread_mat(g)
        lo, hi = g * wide, (g + 1) * wide

        def round_(b, carry, g=g, mat=mat, lo=lo, hi=hi):
            here = pl.ds(pl.multiple_of(b * L, L), L)
            conv(cpad, kc_ref, cc, b, g * STATE)
            c = cc[here, g * STATE : (g + 1) * STATE]
            scores = dot(c, bc[here, g * STATE : (g + 1) * STATE], ((1,), (1,)))
            rowi = lax.broadcasted_iota(jnp.int32, (L, L), 0)
            coli = lax.broadcasted_iota(jnp.int32, (L, L), 1)
            scores = jnp.where(rowi >= coli, scores, 0.0)
            cum = cum_col[here]
            for pair in range(per // 2):
                at = lo + pair * 128
                u = xc[here, at : at + 128]
                parts = []
                for j in range(2):
                    k = g * per + pair * 2 + j
                    gap = jnp.minimum(cum[:, k : k + 1] - cum_row[b, k : k + 1], 0.0)
                    mixing = (scores * jnp.exp(gap) * dt_row[b, k : k + 1]).astype(BF16)
                    parts.append(dot(mixing, u))
                y_v[:, pair * 128 : (pair + 1) * 128] = jnp.where(side, parts[0], parts[1])
            s_hi, s_lo = split(states[b, g])
            inter = dot(c, s_hi) + dot(c, s_lo)
            skip = expand(jnp.broadcast_to(skip_ref[...], (8, heads)), mat)[0:1]
            y = y_v[...] + inter * expand(jnp.exp(cum), mat) + skip * xc[here, lo:hi].astype(F32)
            gated = y * silu(z_v[here, lo:hi].astype(F32))
            power = jnp.mean(gated * gated, axis=-1, keepdims=True)
            normed = gated * lax.rsqrt(power + EPSILON) * gain_ref[:, lo:hi]
            n_all[h, g, here] = normed.astype(BF16)
            r = g * NB + b
            send_own(r)
            forward(r)
            return carry

        lax.fori_loop(0, NB, round_, 0)

    def drain(r, carry):
        forward(r)
        return carry

    lax.fori_loop(R, R + H - 2, drain, 0)

    for k in first + later:
        w_arrived(owner_of(lax.rem(q + NQ - k, NQ), core)).wait_recv()
        w_pair(k).start()
    loads[4].wait()
    for k in [0] + first + later:
        w_arrived(owner_of(lax.rem(q + NQ - k, NQ), 1 - core)).wait_recv()

    end = (h == 0) | (h == H - 1)
    CT = 512

    def unit(r, carry):
        g, b = r // NB, lax.rem(r, NB)
        here = pl.ds(pl.multiple_of(b * L, L), L)
        for d in range(H):
            s = jnp.where(h == 0, d, lax.rem(h + H - d, H))
            if d > 0:

                @pl.when(end)
                def _(s=s):
                    pass_up(s, r).wait_recv()

            def cols(j, c2, d=d, s=s):
                at = pl.ds(pl.multiple_of(j * CT, CT), CT)
                depth = pl.ds(pl.multiple_of((s * G + g) * wide, wide), wide)
                term = dot(n_all[s, g, here], w_all[depth, at])
                if d == 0:

                    @pl.when(g == 0)
                    def _():
                        acc[here, at] = term

                    @pl.when(g > 0)
                    def _():
                        acc[here, at] += term
                elif d == H - 1:
                    total = acc[here, at] + term

                    @pl.when(g < G - 1)
                    def _():
                        acc[here, at] = total

                    @pl.when(g == G - 1)
                    def _():
                        out_ref[0, here, at] = total.astype(BF16)
                else:
                    acc[here, at] += term
                return c2

            lax.fori_loop(0, M // CT, cols, 0)
        return carry

    lax.fori_loop(0, R, unit, 0)

    for copy in halos:

        @pl.when(seq < S - 1)
        def _(copy=copy):
            copy.wait_send()

    for g in range(G):

        @pl.when(seq < S - 1)
        def _(g=g):
            e_copy(g).wait_send()

    for k in first + later:
        w_push(k).wait_send()
    for k in range(NQ):
        w_pair(k).wait_send()

    def sent(r, carry):
        for s in range(H):

            @pl.when((s <= h) & (h < H - 1))
            def _(s=s):
                pass_up(s, r).wait_send()

            @pl.when((s >= h) & (h > 0))
            def _(s=s):
                pass_down(s, r).wait_send()

        return carry

    lax.fori_loop(0, R, sent, 0)


def local(sizes, x_in, b_in, c_in, z_in, dt_in, a_log, skip_gain, norm_gain, conv_x, conv_b, conv_c, init_state, out_weight):
    D, S, H = sizes
    _, T, wide_x = x_in.shape
    wide_b = b_in.shape[2]
    heads = dt_in.shape[1]
    G = wide_b // STATE
    wide = wide_x // G
    NB = T // BLOCK_LEN
    R = G * NB
    rows, M = out_weight.shape
    depth = rows * D * S
    anyw = pl.BlockSpec(memory_space=pl.ANY)
    vmem = pl.BlockSpec(memory_space=pltpu.VMEM)
    dma = pltpu.SemaphoreType.DMA
    return pl.pallas_call(
        functools.partial(kernel, sizes),
        out_shape=jax.ShapeDtypeStruct((1, T, M), BF16),
        in_specs=[anyw] * 5 + [vmem] * 8,
        out_specs=vmem,
        scratch_shapes=[
            pltpu.VMEM((depth, M), BF16),
            pltpu.VMEM((H, G, T, wide), BF16),
            pltpu.VMEM((RIM + T, wide_x), BF16),
            pltpu.VMEM((RIM + T, wide_b), BF16),
            pltpu.VMEM((RIM + T, wide_b), BF16),
            pltpu.VMEM((T, wide_x), BF16),
            pltpu.VMEM((T, wide_x), BF16),
            pltpu.VMEM((T, wide_b), BF16),
            pltpu.VMEM((T, wide_b), BF16),
            pltpu.VMEM((BLOCK_LEN, wide), F32),
            pltpu.VMEM((NB, G, STATE, wide), F32),
            pltpu.VMEM((G, STATE, wide), F32),
            pltpu.VMEM((G, STATE, wide), F32),
            pltpu.VMEM((NB, heads, BLOCK_LEN), F32),
            pltpu.VMEM((NB, heads, BLOCK_LEN), F32),
            pltpu.VMEM((T, heads), F32),
            pltpu.VMEM((T, heads), F32),
            pltpu.VMEM((NB, G, 8, wide), F32),
            pltpu.VMEM((T, M), F32),
            dma((5,)),
            dma((3,)),
            dma((3,)),
            dma((D * S,)),
            dma((D * S,)),
            dma((D * S,)),
            dma((G,)),
            dma((G,)),
            dma((H, R)),
            dma((H, R)),
            dma((H, R)),
        ],
        compiler_params=pltpu.CompilerParams(
            collective_id=0, has_side_effects=True, vmem_limit_bytes=56 * 1024 * 1024
        ),
        cost_estimate=pl.CostEstimate(flops=2 * T * depth * M, bytes_accessed=depth * M * 2, transcendentals=T * wide_x),
    )(
        x_in, b_in, c_in, z_in, out_weight, dt_in,
        a_log.reshape(1, heads), skip_gain.reshape(1, heads), norm_gain.reshape(1, wide_x),
        conv_x, conv_b, conv_c, init_state.reshape(heads * HEAD_SIZE, STATE),
    )


def solution(mesh):
    sizes = (mesh.shape["dp"], mesh.shape["seq"], mesh.shape["head"])
    in_specs = (
        P("dp", "seq", "head"),
        P("dp", "seq", "head"),
        P("dp", "seq", "head"),
        P("dp", "seq", "head"),
        P("dp", "head", "seq"),
        P("head"),
        P("head"),
        P("head"),
        P(None, "head"),
        P(None, "head"),
        P(None, "head"),
        P("dp", "head", None, None),
        P(("dp", "seq"), "head"),
    )
    out_specs = P("dp", "seq", "head")
    return jax.shard_map(
        functools.partial(local, sizes), mesh=mesh, in_specs=in_specs, out_specs=out_specs, check_vma=False
    )
```

```python
import functools

import jax
import jax.numpy as jnp
from jax import lax
from jax.experimental import pallas as pl
from jax.experimental.pallas import tpu as pltpu
from jax.sharding import PartitionSpec as P

HEAD_SIZE = 64
STATE = 128
BLOCK_LEN = 256
TAPS = 4
EPSILON = 1e-05
RIM = 16

F32 = jnp.float32
BF16 = jnp.bfloat16
MESH = pl.DeviceIdType.MESH
HIGHEST = lax.Precision.HIGHEST


def dot(a, b, dims=((1,), (0,)), precision=None):
    return lax.dot_general(a, b, (dims, ((), ())), precision=precision, preferred_element_type=F32)


def split(v):
    hi = v.astype(BF16)
    return hi, (v - hi.astype(F32)).astype(BF16)


def silu(v):
    return v / (1.0 + jnp.exp(-v))


def kernel(
    sizes,
    x_hbm, b_hbm, c_hbm, z_hbm, w_hbm, dt_ref, a_ref, skip_ref, gain_ref, kx_ref, kb_ref, kc_ref, init_ref,
    out_ref,
    w_all, n_all, xpad, bpad, cpad, z_v, xc, bc, cc, y_v, states, e_in, e_out, dt_row, cum_row, dt_col, cum_col,
    decay, acc,
    load_sem, halo_send, halo_recv, wd_send, wc_send, f_send, w_recv, p_send, e_send, e_recv, up_sem, down_sem, n_recv,
):
    D, S, H = sizes
    T = z_v.shape[0]
    G = n_all.shape[1]
    NB = T // BLOCK_LEN
    R = G * NB
    L = BLOCK_LEN
    heads = dt_row.shape[1]
    per = heads // G
    wide = per * HEAD_SIZE
    rows = w_hbm.shape[0]
    M = w_all.shape[1]
    dp, seq, h = lax.axis_index("dp"), lax.axis_index("seq"), lax.axis_index("head")
    SC = S // 2
    core = lax.rem(seq, 2)
    spot = seq // 2
    me = dp * S + seq
    sibling = seq + 1 - 2 * core

    def local(src, dst, i):
        return pltpu.make_async_copy(src, dst, load_sem.at[i])

    loads = [
        local(x_hbm.at[0], xpad.at[pl.ds(RIM, T)], 0),
        local(b_hbm.at[0], bpad.at[pl.ds(RIM, T)], 1),
        local(c_hbm.at[0], cpad.at[pl.ds(RIM, T)], 2),
        local(z_hbm.at[0], z_v, 3),
        local(w_hbm, w_all.at[pl.ds(pl.multiple_of(me * rows, rows), rows)], 4),
    ]
    for copy in loads[:4]:
        copy.start()

    barrier = pltpu.get_barrier_semaphore()
    for k in range(1, D * S):
        other = lax.rem(me + k, D * S)
        pl.semaphore_signal(
            barrier, inc=1, device_id={"dp": other // S, "seq": lax.rem(other, S)}, device_id_type=MESH
        )

    for k in (1, H - 1):
        pl.semaphore_signal(barrier, inc=1, device_id={"head": lax.rem(h + k, H)}, device_id_type=MESH)
    pl.semaphore_wait(barrier, D * S + 1)

    halos = [
        pltpu.make_async_remote_copy(
            src_ref=src.at[0, pl.ds(T - RIM, RIM)],
            dst_ref=dst.at[pl.ds(0, RIM)],
            send_sem=halo_send.at[i],
            recv_sem=halo_recv.at[i],
            device_id={"seq": lax.rem(seq + 1, S)},
            device_id_type=MESH,
        )
        for i, (src, dst) in enumerate(((x_hbm, xpad), (b_hbm, bpad), (c_hbm, cpad)))
    ]
    for copy in halos:

        @pl.when(seq < S - 1)
        def _(copy=copy):
            copy.start()

    half = rows // 2

    def w_rows(owner, part=None):
        if part is None:
            return w_all.at[pl.ds(pl.multiple_of(owner * rows, rows), rows)]
        return w_all.at[pl.ds(pl.multiple_of(owner * rows + part * half, half), half)]

    def row_of(i):
        return lax.rem(dp + D + i, D)

    def spot_of(i):
        return lax.rem(spot + SC + i, SC)

    def owner_of(i, j, on):
        return row_of(-i) * S + spot_of(-j) * 2 + on

    def remote(src, dst, send_sem, recv_sem, device_id):
        return pltpu.make_async_remote_copy(
            src_ref=src, dst_ref=dst, send_sem=send_sem, recv_sem=recv_sem, device_id=device_id, device_id_type=MESH
        )

    def push_dp(i):
        return remote(w_hbm, w_rows(me), wd_send.at[i], w_recv.at[me, 0], {"dp": row_of(i)})

    def push_seq(j):
        return remote(w_hbm, w_rows(me), wc_send.at[j], w_recv.at[me, 0], {"seq": spot_of(j) * 2 + core})

    def hand_seq(i, j):
        owner = owner_of(i, 0, core)
        return remote(
            w_rows(owner, 0), w_rows(owner, 0), f_send.at[0, i, j], w_recv.at[owner, 0],
            {"seq": spot_of(j) * 2 + core},
        )

    def hand_dp(i, j):
        owner = owner_of(0, j, core)
        return remote(
            w_rows(owner, 1), w_rows(owner, 1), f_send.at[1, i, j], w_recv.at[owner, 1], {"dp": row_of(i)}
        )

    def w_pair(i, j, src=None):
        owner = owner_of(i, j, core)
        return remote(
            w_rows(owner) if src is None else src, w_rows(owner), p_send.at[i, j], w_recv.at[owner, 0],
            {"seq": sibling},
        )

    def w_wait(owner, part=None, sem=0):
        ref = w_rows(owner, part)
        remote(ref, ref, p_send.at[0, 0], w_recv.at[owner, sem], {"seq": sibling}).wait_recv()

    for i in range(1, D):
        push_dp(i).start()
    for j in range(1, SC):

        @pl.when(spot_of(j) < spot)
        def _(j=j):
            push_seq(j).start()

    lane = lax.broadcasted_iota(jnp.int32, (L, L), 1)
    line = lax.broadcasted_iota(jnp.int32, (L, L), 0)
    eye = jnp.where(lane == line, 1.0, 0.0).astype(F32)
    low = jnp.where(lane <= line, 1.0, 0.0).astype(F32)
    rate = -jnp.exp(a_ref[...])
    for b in range(NB):
        raw = dt_ref[0, :, b * L : (b + 1) * L]
        step = jnp.maximum(raw, 0.0) + jnp.log1p(jnp.exp(-jnp.abs(raw)))
        dt_row[b] = step
        step_c = dot(eye, step, ((1,), (1,)), HIGHEST)
        cum = dot(low, step_c * rate, precision=HIGHEST)
        dt_col[b * L : (b + 1) * L] = step_c
        cum_col[b * L : (b + 1) * L] = cum
        cum_row[b] = dot(cum, eye, ((0,), (0,)), HIGHEST)

    def spread_mat(g):
        head = lax.broadcasted_iota(jnp.int32, (heads, wide), 0)
        chan = lax.broadcasted_iota(jnp.int32, (heads, wide), 1)
        inside = (chan >= (head - g * per) * HEAD_SIZE) & (chan < (head - g * per + 1) * HEAD_SIZE)
        return jnp.where(inside, 1.0, 0.0).astype(BF16)

    def expand(v, mat):
        hi, lo = split(v)
        return dot(hi, mat) + dot(lo, mat)

    for i in range(3):
        loads[i].wait()
    for copy, pad in zip(halos, (xpad, bpad, cpad)):

        @pl.when(seq > 0)
        def _(copy=copy):
            copy.wait_recv()

        @pl.when(seq == 0)
        def _(pad=pad):
            pad[0:RIM] = jnp.zeros((RIM, pad.shape[1]), BF16)

    def conv(pad, taps, dst, b, at):
        v = pad[pl.ds(pl.multiple_of(b * L, L), L + RIM), at : at + 128].astype(F32)
        total = v * taps[TAPS - 1 : TAPS, at : at + 128]
        for back in range(1, TAPS):
            total = total + pltpu.roll(v, back, 0) * taps[TAPS - 1 - back : TAPS - back, at : at + 128]
        dst[pl.ds(pl.multiple_of(b * L, L), L), at : at + 128] = silu(total[RIM:]).astype(BF16)

    def e_copy(g):
        return pltpu.make_async_remote_copy(
            src_ref=e_out.at[g],
            dst_ref=e_in.at[g],
            send_sem=e_send.at[g],
            recv_sem=e_recv.at[g],
            device_id={"seq": lax.rem(seq + 1, S)},
            device_id_type=MESH,
        )

    for g in range(G):
        mat = spread_mat(g)

        def block(b, carry, g=g, mat=mat):
            here = pl.ds(pl.multiple_of(b * L, L), L)
            conv(bpad, kb_ref, bc, b, g * STATE)
            for at in range(g * wide, (g + 1) * wide, 128):
                conv(xpad, kx_ref, xc, b, at)
            cum = cum_col[here]
            last = cum[L - 1 : L]
            weight = expand(jnp.exp(last - cum) * dt_col[here], mat)
            weighted = (weight * xc[here, g * wide : (g + 1) * wide].astype(F32)).astype(BF16)
            states[b, g] = dot(bc[here, g * STATE : (g + 1) * STATE], weighted, ((0,), (0,)))
            decay[b, g] = expand(jnp.broadcast_to(jnp.exp(last), (8, heads)), mat)
            return carry

        lax.fori_loop(0, NB, block, 0)

        @pl.when(seq == 0)
        def _(g=g):
            e_in[g] = init_ref[g * wide : (g + 1) * wide].T

        @pl.when(seq > 0)
        def _(g=g):
            e_copy(g).wait_recv()

        def chain(i, carry, g=g):
            at = pl.ds(pl.multiple_of(i * 32, 32), 32)
            run = e_in[g, at]
            for b in range(NB):
                fresh = states[b, g, at]
                states[b, g, at] = run
                run = decay[b, g, 0:1] * run + fresh
            e_out[g, at] = run
            return carry

        lax.fori_loop(0, STATE // 32, chain, 0)

        @pl.when(seq < S - 1)
        def _(g=g):
            e_copy(g).start()

    for j in range(1, SC):

        @pl.when(spot_of(j) > spot)
        def _(j=j):
            push_seq(j).start()

    w_pair(0, 0, w_hbm).start()
    loads[4].start()

    def chunk(s, r):
        return n_all.at[s, r // NB, pl.ds(pl.multiple_of(lax.rem(r, NB) * L, L), L)]

    def pass_up(s, r):
        return pltpu.make_async_remote_copy(
            src_ref=chunk(s, r), dst_ref=chunk(s, r), send_sem=up_sem.at[s, r], recv_sem=n_recv.at[s, r],
            device_id={"head": lax.rem(h + 1, H)}, device_id_type=MESH,
        )

    def pass_down(s, r):
        return pltpu.make_async_remote_copy(
            src_ref=chunk(s, r), dst_ref=chunk(s, r), send_sem=down_sem.at[s, r], recv_sem=n_recv.at[s, r],
            device_id={"head": lax.rem(h + H - 1, H)}, device_id_type=MESH,
        )

    def send_own(r):
        @pl.when(h < H - 1)
        def _():
            pass_up(h, r).start()

        @pl.when(h > 0)
        def _():
            pass_down(h, r).start()

    def arrive(d, r, side):
        s = h - d if side < 0 else h + d
        copy = (pass_up if side < 0 else pass_down)(s, r)
        copy.wait_recv()

        @pl.when((h < H - 1) if side < 0 else (h > 0))
        def _():
            copy.start()

    def exists(d, side):
        return (h - d >= 0) if side < 0 else (h + d < H)

    loads[3].wait()
    side = lax.broadcasted_iota(jnp.int32, (L, 128), 1) < HEAD_SIZE
    for g in range(G):
        mat = spread_mat(g)
        lo, hi = g * wide, (g + 1) * wide

        def round_(b, carry, g=g, mat=mat, lo=lo, hi=hi):
            here = pl.ds(pl.multiple_of(b * L, L), L)
            conv(cpad, kc_ref, cc, b, g * STATE)
            c = cc[here, g * STATE : (g + 1) * STATE]
            scores = dot(c, bc[here, g * STATE : (g + 1) * STATE], ((1,), (1,)))
            rowi = lax.broadcasted_iota(jnp.int32, (L, L), 0)
            coli = lax.broadcasted_iota(jnp.int32, (L, L), 1)
            scores = jnp.where(rowi >= coli, scores, 0.0)
            cum = cum_col[here]
            for pair in range(per // 2):
                at = lo + pair * 128
                u = xc[here, at : at + 128]
                parts = []
                for j in range(2):
                    k = g * per + pair * 2 + j
                    gap = jnp.minimum(cum[:, k : k + 1] - cum_row[b, k : k + 1], 0.0)
                    mixing = (scores * jnp.exp(gap) * dt_row[b, k : k + 1]).astype(BF16)
                    parts.append(dot(mixing, u))
                y_v[:, pair * 128 : (pair + 1) * 128] = jnp.where(side, parts[0], parts[1])
            s_hi, s_lo = split(states[b, g])
            inter = dot(c, s_hi) + dot(c, s_lo)
            skip = expand(jnp.broadcast_to(skip_ref[...], (8, heads)), mat)[0:1]
            y = y_v[...] + inter * expand(jnp.exp(cum), mat) + skip * xc[here, lo:hi].astype(F32)
            gated = y * silu(z_v[here, lo:hi].astype(F32))
            power = jnp.mean(gated * gated, axis=-1, keepdims=True)
            normed = gated * lax.rsqrt(power + EPSILON) * gain_ref[:, lo:hi]
            n_all[h, g, here] = normed.astype(BF16)
            r = g * NB + b
            send_own(r)
            return carry

        lax.fori_loop(0, NB, round_, 0)

    for i in range(1, D):
        w_wait(owner_of(i, 0, core))
        for j in range(1, SC):
            hand_seq(i, j).start()
        w_pair(i, 0).start()
    for j in range(1, SC):
        w_wait(owner_of(0, j, core))
        for i in range(1, D):
            hand_dp(i, j).start()
        w_pair(0, j).start()

    def nearest(r, carry):
        for side in (-1, 1):

            @pl.when(exists(1, side))
            def _(side=side):
                arrive(1, r, side)

        return carry

    lax.fori_loop(0, R, nearest, 0)

    for i in range(1, D):
        for j in range(1, SC):
            owner = owner_of(i, j, core)
            w_wait(owner, 0, 0)
            w_wait(owner, 1, 1)
            w_pair(i, j).start()
    loads[4].wait()
    for i in range(D):
        for j in range(SC):
            w_wait(owner_of(i, j, 1 - core))

    CT = 512

    def product(s, r, fresh=False):
        g = r // NB
        here = pl.ds(pl.multiple_of(lax.rem(r, NB) * L, L), L)
        depth = pl.ds(pl.multiple_of((s * G + g) * wide, wide), wide)

        def cols(j, carry):
            at = pl.ds(pl.multiple_of(j * CT, CT), CT)
            term = dot(n_all[s, g, here], w_all[depth, at])
            if not fresh:
                acc[here, at] += term
            else:

                @pl.when(g == 0)
                def _():
                    acc[here, at] = term

                @pl.when(g > 0)
                def _():
                    acc[here, at] += term

            return carry

        lax.fori_loop(0, M // CT, cols, 0)

    def near(r, carry):
        product(h, r, True)
        for d in range(1, H - 1):
            for side in (-1, 1):

                @pl.when(exists(d, side))
                def _(d=d, side=side):
                    if d > 1:
                        arrive(d, r, side)
                    product(h + side * d, r)

        return carry

    lax.fori_loop(0, R, near, 0)

    def far(r, carry):
        for side in (-1, 1):

            @pl.when(exists(H - 1, side))
            def _(side=side):
                if H > 2:
                    arrive(H - 1, r, side)
                product(h + side * (H - 1), r)

        @pl.when(r >= R - NB)
        def _():
            here = pl.ds(pl.multiple_of(lax.rem(r, NB) * L, L), L)
            for at in range(0, M, CT):
                out_ref[0, here, at : at + CT] = acc[here, at : at + CT].astype(BF16)

        return carry

    lax.fori_loop(0, R, far, 0)

    for copy in halos:

        @pl.when(seq < S - 1)
        def _(copy=copy):
            copy.wait_send()

    for g in range(G):

        @pl.when(seq < S - 1)
        def _(g=g):
            e_copy(g).wait_send()

    for i in range(D):
        for j in range(SC):
            w_pair(i, j).wait_send()
            if i > 0 and j > 0:
                hand_seq(i, j).wait_send()
                hand_dp(i, j).wait_send()
    for i in range(1, D):
        push_dp(i).wait_send()
    for j in range(1, SC):
        push_seq(j).wait_send()

    def sent(r, carry):
        for s in range(H):

            @pl.when((s <= h) & (h < H - 1))
            def _(s=s):
                pass_up(s, r).wait_send()

            @pl.when((s >= h) & (h > 0))
            def _(s=s):
                pass_down(s, r).wait_send()

        return carry

    lax.fori_loop(0, R, sent, 0)


def local(sizes, x_in, b_in, c_in, z_in, dt_in, a_log, skip_gain, norm_gain, conv_x, conv_b, conv_c, init_state, out_weight):
    D, S, H = sizes
    _, T, wide_x = x_in.shape
    wide_b = b_in.shape[2]
    heads = dt_in.shape[1]
    G = wide_b // STATE
    wide = wide_x // G
    NB = T // BLOCK_LEN
    R = G * NB
    rows, M = out_weight.shape
    depth = rows * D * S
    anyw = pl.BlockSpec(memory_space=pl.ANY)
    vmem = pl.BlockSpec(memory_space=pltpu.VMEM)
    dma = pltpu.SemaphoreType.DMA
    return pl.pallas_call(
        functools.partial(kernel, sizes),
        out_shape=jax.ShapeDtypeStruct((1, T, M), BF16),
        in_specs=[anyw] * 5 + [vmem] * 8,
        out_specs=vmem,
        scratch_shapes=[
            pltpu.VMEM((depth, M), BF16),
            pltpu.VMEM((H, G, T, wide), BF16),
            pltpu.VMEM((RIM + T, wide_x), BF16),
            pltpu.VMEM((RIM + T, wide_b), BF16),
            pltpu.VMEM((RIM + T, wide_b), BF16),
            pltpu.VMEM((T, wide_x), BF16),
            pltpu.VMEM((T, wide_x), BF16),
            pltpu.VMEM((T, wide_b), BF16),
            pltpu.VMEM((T, wide_b), BF16),
            pltpu.VMEM((BLOCK_LEN, wide), F32),
            pltpu.VMEM((NB, G, STATE, wide), F32),
            pltpu.VMEM((G, STATE, wide), F32),
            pltpu.VMEM((G, STATE, wide), F32),
            pltpu.VMEM((NB, heads, BLOCK_LEN), F32),
            pltpu.VMEM((NB, heads, BLOCK_LEN), F32),
            pltpu.VMEM((T, heads), F32),
            pltpu.VMEM((T, heads), F32),
            pltpu.VMEM((NB, G, 8, wide), F32),
            pltpu.VMEM((T, M), F32),
            dma((5,)),
            dma((3,)),
            dma((3,)),
            dma((D,)),
            dma((S // 2,)),
            dma((2, D, S // 2)),
            dma((D * S, 2)),
            dma((D, S // 2)),
            dma((G,)),
            dma((G,)),
            dma((H, R)),
            dma((H, R)),
            dma((H, R)),
        ],
        compiler_params=pltpu.CompilerParams(
            collective_id=0, has_side_effects=True, vmem_limit_bytes=56 * 1024 * 1024
        ),
        cost_estimate=pl.CostEstimate(flops=2 * T * depth * M, bytes_accessed=depth * M * 2, transcendentals=T * wide_x),
    )(
        x_in, b_in, c_in, z_in, out_weight, dt_in,
        a_log.reshape(1, heads), skip_gain.reshape(1, heads), norm_gain.reshape(1, wide_x),
        conv_x, conv_b, conv_c, init_state.reshape(heads * HEAD_SIZE, STATE),
    )


def solution(mesh):
    sizes = (mesh.shape["dp"], mesh.shape["seq"], mesh.shape["head"])
    in_specs = (
        P("dp", "seq", "head"),
        P("dp", "seq", "head"),
        P("dp", "seq", "head"),
        P("dp", "seq", "head"),
        P("dp", "head", "seq"),
        P("head"),
        P("head"),
        P("head"),
        P(None, "head"),
        P(None, "head"),
        P(None, "head"),
        P("dp", "head", None, None),
        P(("dp", "seq"), "head"),
    )
    out_specs = P("dp", "seq", "head")
    return jax.shard_map(
        functools.partial(local, sizes), mesh=mesh, in_specs=in_specs, out_specs=out_specs, check_vma=False
    )
```

```python
import functools

import jax
import jax.numpy as jnp
from jax import lax
from jax.experimental import pallas as pl
from jax.experimental.pallas import tpu as pltpu
from jax.sharding import PartitionSpec as P

HEAD_SIZE = 64
STATE = 128
BLOCK_LEN = 256
TAPS = 4
EPSILON = 1e-05
RIM = 16

F32 = jnp.float32
BF16 = jnp.bfloat16
MESH = pl.DeviceIdType.MESH
HIGHEST = lax.Precision.HIGHEST


def dot(a, b, dims=((1,), (0,)), precision=None):
    return lax.dot_general(a, b, (dims, ((), ())), precision=precision, preferred_element_type=F32)


def split(v):
    hi = v.astype(BF16)
    return hi, (v - hi.astype(F32)).astype(BF16)


def silu(v):
    return v / (1.0 + jnp.exp(-v))


def kernel(
    sizes,
    x_hbm, b_hbm, c_hbm, z_hbm, w_hbm, dt_ref, a_ref, skip_ref, gain_ref, kx_ref, kb_ref, kc_ref, init_ref,
    out_ref,
    w_all, n_all, xpad, bpad, cpad, z_v, xc, bc, cc, y_v, states, e_in, e_out, dt_row, cum_row, dt_col, cum_col,
    decay, acc,
    load_sem, halo_send, halo_recv, wd_send, wc_send, f_send, w_recv, p_send, e_send, e_recv, up_sem, down_sem, n_recv,
):
    D, S, H = sizes
    T = z_v.shape[0]
    G = n_all.shape[1]
    NB = T // BLOCK_LEN
    R = G * NB
    L = BLOCK_LEN
    heads = dt_row.shape[1]
    per = heads // G
    wide = per * HEAD_SIZE
    rows = w_hbm.shape[0]
    M = w_all.shape[1]
    dp, seq, h = lax.axis_index("dp"), lax.axis_index("seq"), lax.axis_index("head")
    SC = S // 2
    core = lax.rem(seq, 2)
    spot = seq // 2
    me = dp * S + seq
    sibling = seq + 1 - 2 * core

    def local(src, dst, i):
        return pltpu.make_async_copy(src, dst, load_sem.at[i])

    loads = [
        local(x_hbm.at[0], xpad.at[pl.ds(RIM, T)], 0),
        local(b_hbm.at[0], bpad.at[pl.ds(RIM, T)], 1),
        local(c_hbm.at[0], cpad.at[pl.ds(RIM, T)], 2),
        local(z_hbm.at[0], z_v, 3),
        local(w_hbm, w_all.at[pl.ds(pl.multiple_of(me * rows, rows), rows)], 4),
    ]
    for copy in loads[:4]:
        copy.start()

    barrier = pltpu.get_barrier_semaphore()
    for k in range(1, D * S):
        other = lax.rem(me + k, D * S)
        pl.semaphore_signal(
            barrier, inc=1, device_id={"dp": other // S, "seq": lax.rem(other, S)}, device_id_type=MESH
        )

    for k in (1, H - 1):
        pl.semaphore_signal(barrier, inc=1, device_id={"head": lax.rem(h + k, H)}, device_id_type=MESH)
    pl.semaphore_wait(barrier, D * S + 1)

    halos = [
        pltpu.make_async_remote_copy(
            src_ref=src.at[0, pl.ds(T - RIM, RIM)],
            dst_ref=dst.at[pl.ds(0, RIM)],
            send_sem=halo_send.at[i],
            recv_sem=halo_recv.at[i],
            device_id={"seq": lax.rem(seq + 1, S)},
            device_id_type=MESH,
        )
        for i, (src, dst) in enumerate(((x_hbm, xpad), (b_hbm, bpad), (c_hbm, cpad)))
    ]
    for copy in halos:

        @pl.when(seq < S - 1)
        def _(copy=copy):
            copy.start()

    half = rows // 2

    def w_rows(owner, part=None):
        if part is None:
            return w_all.at[pl.ds(pl.multiple_of(owner * rows, rows), rows)]
        return w_all.at[pl.ds(pl.multiple_of(owner * rows + part * half, half), half)]

    def row_of(i):
        return lax.rem(dp + D + i, D)

    def spot_of(i):
        return lax.rem(spot + SC + i, SC)

    def owner_of(i, j, on):
        return row_of(-i) * S + spot_of(-j) * 2 + on

    def remote(src, dst, send_sem, recv_sem, device_id):
        return pltpu.make_async_remote_copy(
            src_ref=src, dst_ref=dst, send_sem=send_sem, recv_sem=recv_sem, device_id=device_id, device_id_type=MESH
        )

    def push_dp(i):
        return remote(w_hbm, w_rows(me), wd_send.at[i], w_recv.at[me, 0], {"dp": row_of(i)})

    def push_seq(j):
        return remote(w_hbm, w_rows(me), wc_send.at[j], w_recv.at[me, 0], {"seq": spot_of(j) * 2 + core})

    def hand_seq(i, j):
        owner = owner_of(i, 0, core)
        return remote(
            w_rows(owner, 0), w_rows(owner, 0), f_send.at[0, i, j], w_recv.at[owner, 0],
            {"seq": spot_of(j) * 2 + core},
        )

    def hand_dp(i, j):
        owner = owner_of(0, j, core)
        return remote(
            w_rows(owner, 1), w_rows(owner, 1), f_send.at[1, i, j], w_recv.at[owner, 1], {"dp": row_of(i)}
        )

    def w_pair(i, j, src=None):
        owner = owner_of(i, j, core)
        return remote(
            w_rows(owner) if src is None else src, w_rows(owner), p_send.at[i, j], w_recv.at[owner, 0],
            {"seq": sibling},
        )

    def w_wait(owner, part=None, sem=0):
        ref = w_rows(owner, part)
        remote(ref, ref, p_send.at[0, 0], w_recv.at[owner, sem], {"seq": sibling}).wait_recv()

    for i in range(1, D):
        push_dp(i).start()
    for j in range(1, SC):

        @pl.when(spot_of(j) < spot)
        def _(j=j):
            push_seq(j).start()

    lane = lax.broadcasted_iota(jnp.int32, (L, L), 1)
    line = lax.broadcasted_iota(jnp.int32, (L, L), 0)
    eye = jnp.where(lane == line, 1.0, 0.0).astype(F32)
    low = jnp.where(lane <= line, 1.0, 0.0).astype(F32)
    rate = -jnp.exp(a_ref[...])
    for b in range(NB):
        raw = dt_ref[0, :, b * L : (b + 1) * L]
        step = jnp.maximum(raw, 0.0) + jnp.log1p(jnp.exp(-jnp.abs(raw)))
        dt_row[b] = step
        step_c = dot(eye, step, ((1,), (1,)), HIGHEST)
        cum = dot(low, step_c * rate, precision=HIGHEST)
        dt_col[b * L : (b + 1) * L] = step_c
        cum_col[b * L : (b + 1) * L] = cum
        cum_row[b] = dot(cum, eye, ((0,), (0,)), HIGHEST)

    def spread_mat(g):
        head = lax.broadcasted_iota(jnp.int32, (heads, wide), 0)
        chan = lax.broadcasted_iota(jnp.int32, (heads, wide), 1)
        inside = (chan >= (head - g * per) * HEAD_SIZE) & (chan < (head - g * per + 1) * HEAD_SIZE)
        return jnp.where(inside, 1.0, 0.0).astype(BF16)

    def expand(v, mat):
        hi, lo = split(v)
        return dot(hi, mat) + dot(lo, mat)

    for i in range(3):
        loads[i].wait()
    for copy, pad in zip(halos, (xpad, bpad, cpad)):

        @pl.when(seq > 0)
        def _(copy=copy):
            copy.wait_recv()

        @pl.when(seq == 0)
        def _(pad=pad):
            pad[0:RIM] = jnp.zeros((RIM, pad.shape[1]), BF16)

    def conv(pad, taps, dst, b, at):
        v = pad[pl.ds(pl.multiple_of(b * L, L), L + RIM), at : at + 128].astype(F32)
        total = v * taps[TAPS - 1 : TAPS, at : at + 128]
        for back in range(1, TAPS):
            total = total + pltpu.roll(v, back, 0) * taps[TAPS - 1 - back : TAPS - back, at : at + 128]
        dst[pl.ds(pl.multiple_of(b * L, L), L), at : at + 128] = silu(total[RIM:]).astype(BF16)

    def e_copy(g):
        return pltpu.make_async_remote_copy(
            src_ref=e_out.at[g],
            dst_ref=e_in.at[g],
            send_sem=e_send.at[g],
            recv_sem=e_recv.at[g],
            device_id={"seq": lax.rem(seq + 1, S)},
            device_id_type=MESH,
        )

    def chunk(s, r):
        return n_all.at[s, r // NB, pl.ds(pl.multiple_of(lax.rem(r, NB) * L, L), L)]

    def pass_up(s, r):
        return pltpu.make_async_remote_copy(
            src_ref=chunk(s, r), dst_ref=chunk(s, r), send_sem=up_sem.at[s, r], recv_sem=n_recv.at[s, r],
            device_id={"head": lax.rem(h + 1, H)}, device_id_type=MESH,
        )

    def pass_down(s, r):
        return pltpu.make_async_remote_copy(
            src_ref=chunk(s, r), dst_ref=chunk(s, r), send_sem=down_sem.at[s, r], recv_sem=n_recv.at[s, r],
            device_id={"head": lax.rem(h + H - 1, H)}, device_id_type=MESH,
        )

    def send_own(r):
        @pl.when(h < H - 1)
        def _():
            pass_up(h, r).start()

        @pl.when(h > 0)
        def _():
            pass_down(h, r).start()

    def arrive(d, r, side):
        s = h - d if side < 0 else h + d
        copy = (pass_up if side < 0 else pass_down)(s, r)
        copy.wait_recv()

        @pl.when((h < H - 1) if side < 0 else (h > 0))
        def _():
            copy.start()

    def exists(d, side):
        return (h - d >= 0) if side < 0 else (h + d < H)

    loads[3].wait()
    side = lax.broadcasted_iota(jnp.int32, (L, 128), 1) < HEAD_SIZE
    for g in range(G):
        mat = spread_mat(g)

        def block(b, carry, g=g, mat=mat):
            here = pl.ds(pl.multiple_of(b * L, L), L)
            conv(bpad, kb_ref, bc, b, g * STATE)
            for at in range(g * wide, (g + 1) * wide, 128):
                conv(xpad, kx_ref, xc, b, at)
            cum = cum_col[here]
            last = cum[L - 1 : L]
            weight = expand(jnp.exp(last - cum) * dt_col[here], mat)
            weighted = (weight * xc[here, g * wide : (g + 1) * wide].astype(F32)).astype(BF16)
            states[b, g] = dot(bc[here, g * STATE : (g + 1) * STATE], weighted, ((0,), (0,)))
            decay[b, g] = expand(jnp.broadcast_to(jnp.exp(last), (8, heads)), mat)
            return carry

        lax.fori_loop(0, NB, block, 0)

        @pl.when(seq == 0)
        def _(g=g):
            e_in[g] = init_ref[g * wide : (g + 1) * wide].T

        @pl.when(seq > 0)
        def _(g=g):
            e_copy(g).wait_recv()

        def chain(i, carry, g=g):
            at = pl.ds(pl.multiple_of(i * 32, 32), 32)
            run = e_in[g, at]
            for b in range(NB):
                fresh = states[b, g, at]
                states[b, g, at] = run
                run = decay[b, g, 0:1] * run + fresh
            e_out[g, at] = run
            return carry

        lax.fori_loop(0, STATE // 32, chain, 0)

        @pl.when(seq < S - 1)
        def _(g=g):
            e_copy(g).start()

        lo, hi = g * wide, (g + 1) * wide

        def round_(b, carry, g=g, mat=mat, lo=lo, hi=hi):
            here = pl.ds(pl.multiple_of(b * L, L), L)
            conv(cpad, kc_ref, cc, b, g * STATE)
            c = cc[here, g * STATE : (g + 1) * STATE]
            scores = dot(c, bc[here, g * STATE : (g + 1) * STATE], ((1,), (1,)))
            rowi = lax.broadcasted_iota(jnp.int32, (L, L), 0)
            coli = lax.broadcasted_iota(jnp.int32, (L, L), 1)
            scores = jnp.where(rowi >= coli, scores, 0.0)
            cum = cum_col[here]
            for pair in range(per // 2):
                at = lo + pair * 128
                u = xc[here, at : at + 128]
                parts = []
                for j in range(2):
                    k = g * per + pair * 2 + j
                    gap = jnp.minimum(cum[:, k : k + 1] - cum_row[b, k : k + 1], 0.0)
                    mixing = (scores * jnp.exp(gap) * dt_row[b, k : k + 1]).astype(BF16)
                    parts.append(dot(mixing, u))
                y_v[:, pair * 128 : (pair + 1) * 128] = jnp.where(side, parts[0], parts[1])
            s_hi, s_lo = split(states[b, g])
            inter = dot(c, s_hi) + dot(c, s_lo)
            skip = expand(jnp.broadcast_to(skip_ref[...], (8, heads)), mat)[0:1]
            y = y_v[...] + inter * expand(jnp.exp(cum), mat) + skip * xc[here, lo:hi].astype(F32)
            gated = y * silu(z_v[here, lo:hi].astype(F32))
            power = jnp.mean(gated * gated, axis=-1, keepdims=True)
            normed = gated * lax.rsqrt(power + EPSILON) * gain_ref[:, lo:hi]
            n_all[h, g, here] = normed.astype(BF16)
            r = g * NB + b
            send_own(r)
            return carry

        lax.fori_loop(0, NB, round_, 0)

        if g == 0:
            for j in range(1, SC):

                @pl.when(spot_of(j) > spot)
                def _(j=j):
                    push_seq(j).start()

            w_pair(0, 0, w_hbm).start()
            loads[4].start()

    for i in range(1, D):
        w_wait(owner_of(i, 0, core))
        for j in range(1, SC):
            hand_seq(i, j).start()
        w_pair(i, 0).start()
    def nearest(r, carry):
        for side in (-1, 1):

            @pl.when(exists(1, side))
            def _(side=side):
                arrive(1, r, side)

        return carry

    lax.fori_loop(0, R, nearest, 0)

    for j in range(1, SC):
        w_wait(owner_of(0, j, core))
        for i in range(1, D):
            hand_dp(i, j).start()
        w_pair(0, j).start()

    for i in range(1, D):
        for j in range(1, SC):
            owner = owner_of(i, j, core)
            w_wait(owner, 0, 0)
            w_wait(owner, 1, 1)
            w_pair(i, j).start()
    loads[4].wait()
    for i in range(D):
        for j in range(SC):
            w_wait(owner_of(i, j, 1 - core))

    CT = 512

    def product(s, g, here, CT, fresh=False):
        depth = pl.ds(pl.multiple_of((s * G + g) * wide, wide), wide)

        def cols(j, carry):
            at = pl.ds(pl.multiple_of(j * CT, CT), CT)
            term = dot(n_all[s, g, here], w_all[depth, at])
            if not fresh:
                acc[here, at] += term
            else:

                @pl.when(g == 0)
                def _():
                    acc[here, at] = term

                @pl.when(g > 0)
                def _():
                    acc[here, at] += term

            return carry

        lax.fori_loop(0, M // CT, cols, 0)

    def near(g, carry):
        here = pl.ds(0, T)
        product(h, g, here, 256, True)
        for d in range(1, H - 1):
            for side in (-1, 1):

                @pl.when(exists(d, side))
                def _(d=d, side=side):
                    if d > 1:
                        for b in range(NB):
                            arrive(d, g * NB + b, side)
                    product(h + side * d, g, here, 256)

        return carry

    lax.fori_loop(0, G, near, 0)

    def far(r, carry):
        here = pl.ds(pl.multiple_of(lax.rem(r, NB) * L, L), L)
        for side in (-1, 1):

            @pl.when(exists(H - 1, side))
            def _(side=side):
                if H > 2:
                    arrive(H - 1, r, side)
                product(h + side * (H - 1), r // NB, here, CT)

        @pl.when(r >= R - NB)
        def _():
            for at in range(0, M, CT):
                out_ref[0, here, at : at + CT] = acc[here, at : at + CT].astype(BF16)

        return carry

    lax.fori_loop(0, R, far, 0)

    for copy in halos:

        @pl.when(seq < S - 1)
        def _(copy=copy):
            copy.wait_send()

    for g in range(G):

        @pl.when(seq < S - 1)
        def _(g=g):
            e_copy(g).wait_send()

    for i in range(D):
        for j in range(SC):
            w_pair(i, j).wait_send()
            if i > 0 and j > 0:
                hand_seq(i, j).wait_send()
                hand_dp(i, j).wait_send()
    for i in range(1, D):
        push_dp(i).wait_send()
    for j in range(1, SC):
        push_seq(j).wait_send()

    def sent(r, carry):
        for s in range(H):

            @pl.when((s <= h) & (h < H - 1))
            def _(s=s):
                pass_up(s, r).wait_send()

            @pl.when((s >= h) & (h > 0))
            def _(s=s):
                pass_down(s, r).wait_send()

        return carry

    lax.fori_loop(0, R, sent, 0)


def local(sizes, x_in, b_in, c_in, z_in, dt_in, a_log, skip_gain, norm_gain, conv_x, conv_b, conv_c, init_state, out_weight):
    D, S, H = sizes
    _, T, wide_x = x_in.shape
    wide_b = b_in.shape[2]
    heads = dt_in.shape[1]
    G = wide_b // STATE
    wide = wide_x // G
    NB = T // BLOCK_LEN
    R = G * NB
    rows, M = out_weight.shape
    depth = rows * D * S
    anyw = pl.BlockSpec(memory_space=pl.ANY)
    vmem = pl.BlockSpec(memory_space=pltpu.VMEM)
    dma = pltpu.SemaphoreType.DMA
    return pl.pallas_call(
        functools.partial(kernel, sizes),
        out_shape=jax.ShapeDtypeStruct((1, T, M), BF16),
        in_specs=[anyw] * 5 + [vmem] * 8,
        out_specs=vmem,
        scratch_shapes=[
            pltpu.VMEM((depth, M), BF16),
            pltpu.VMEM((H, G, T, wide), BF16),
            pltpu.VMEM((RIM + T, wide_x), BF16),
            pltpu.VMEM((RIM + T, wide_b), BF16),
            pltpu.VMEM((RIM + T, wide_b), BF16),
            pltpu.VMEM((T, wide_x), BF16),
            pltpu.VMEM((T, wide_x), BF16),
            pltpu.VMEM((T, wide_b), BF16),
            pltpu.VMEM((T, wide_b), BF16),
            pltpu.VMEM((BLOCK_LEN, wide), F32),
            pltpu.VMEM((NB, G, STATE, wide), F32),
            pltpu.VMEM((G, STATE, wide), F32),
            pltpu.VMEM((G, STATE, wide), F32),
            pltpu.VMEM((NB, heads, BLOCK_LEN), F32),
            pltpu.VMEM((NB, heads, BLOCK_LEN), F32),
            pltpu.VMEM((T, heads), F32),
            pltpu.VMEM((T, heads), F32),
            pltpu.VMEM((NB, G, 8, wide), F32),
            pltpu.VMEM((T, M), F32),
            dma((5,)),
            dma((3,)),
            dma((3,)),
            dma((D,)),
            dma((S // 2,)),
            dma((2, D, S // 2)),
            dma((D * S, 2)),
            dma((D, S // 2)),
            dma((G,)),
            dma((G,)),
            dma((H, R)),
            dma((H, R)),
            dma((H, R)),
        ],
        compiler_params=pltpu.CompilerParams(
            collective_id=0, has_side_effects=True, vmem_limit_bytes=56 * 1024 * 1024
        ),
        cost_estimate=pl.CostEstimate(flops=2 * T * depth * M, bytes_accessed=depth * M * 2, transcendentals=T * wide_x),
    )(
        x_in, b_in, c_in, z_in, out_weight, dt_in,
        a_log.reshape(1, heads), skip_gain.reshape(1, heads), norm_gain.reshape(1, wide_x),
        conv_x, conv_b, conv_c, init_state.reshape(heads * HEAD_SIZE, STATE),
    )


def solution(mesh):
    sizes = (mesh.shape["dp"], mesh.shape["seq"], mesh.shape["head"])
    in_specs = (
        P("dp", "seq", "head"),
        P("dp", "seq", "head"),
        P("dp", "seq", "head"),
        P("dp", "seq", "head"),
        P("dp", "head", "seq"),
        P("head"),
        P("head"),
        P("head"),
        P(None, "head"),
        P(None, "head"),
        P(None, "head"),
        P("dp", "head", None, None),
        P(("dp", "seq"), "head"),
    )
    out_specs = P("dp", "seq", "head")
    return jax.shard_map(
        functools.partial(local, sizes), mesh=mesh, in_specs=in_specs, out_specs=out_specs, check_vma=False
    )
```
